32 devices in a mesh: row: 8 (over z, core), col: 4 (over y, x).
Axes of the slice: x: 2, y: 2, z: 4, core: 2. Of those that a mesh axis runs over, the one named last changes fastest.
Arguments:
- blocks: bfloat16 [8, 4, 5, 128, 8192], P('row', 'col'), may hold values from -6 to 6
- coords: int32 [8, 4, 5, 3], P('row', 'col'), may hold values from 0 to 7, as said below
- counts: int32 [8, 4], P('row', 'col'), may hold values from 1 to 5, as said below
- doc_factor: bfloat16 [4096, 128], P(('col', 'row')), may hold values from -6 to 6
- ctx_factor: bfloat16 [512, 128], P('col'), may hold values from -0.0625 to 0.0625
Outputs:
- mttkrp: float32 [4096, 128], P(('row', 'col'))
The draws below stay inside these ranges and needn't reach their ends.
Inputs may be any that keep to these rules, and one draw needn't show every extreme that they name: coords[..., 0] lies in 0 to 3, coords[..., 1] in 0 to 7, coords[..., 2] in 0 to 7; slots at or past the device's count are ignored. `counts`: some device uses all 5 slots.
All inputs are finite; a program needn't handle non-finite values.
Results may differ from the reference program's by a relative error of at most 0.0029.
Values may be sent and summed in bfloat16 or wider, within the bound.
A program may use at most 64 MiB of HBM per device.

```python
import jax
import jax.numpy as jnp
from jax import lax

R = 128
BQ = 128
BD = 128
BK = 64
KB = 8
NB_DEV = 5
QBC = 1
DBC = 1
RGROUPS = 8
CGROUPS = 4
QB_ROW = 4
DB_COL = 8
QUERIES = 4096
DOCS = 4096
CTX = 512


def draw_coords(key, part):
    keys = jax.random.split(key, 3)
    shape = (RGROUPS, CGROUPS, NB_DEV)
    query_ids = jax.random.randint(keys[0], shape, 0, QBC * CGROUPS)
    doc_ids = jax.random.randint(keys[1], shape, 0, DBC * RGROUPS)
    ctx_ids = jax.random.randint(keys[2], shape, 0, KB)
    return jnp.stack([query_ids, doc_ids, ctx_ids], axis=-1).astype(jnp.int32)


def draw_counts(key, part):
    keys = jax.random.split(key, 3)
    shape = (RGROUPS, CGROUPS)
    light = jax.random.randint(keys[0], shape, 1, 3)
    heavy = jax.random.randint(keys[1], shape, 0, 4) == 0
    values = jnp.where(heavy, NB_DEV, light).reshape(-1)
    chosen = jax.random.randint(keys[2], (), 0, RGROUPS * CGROUPS)
    values = values.at[chosen].set(NB_DEV)
    return values.reshape(shape).astype(jnp.int32)


def levels(key, shape, pieces, smallest, top_value):
    gain, own = 1.0, jax.random.fold_in(key, 6)
    for dim, blocks in pieces:
        steps = jnp.exp(jax.random.uniform(jax.random.fold_in(own, dim), (blocks,), jnp.float32, smallest / len(pieces), top_value / len(pieces)))
        gain = gain * jnp.repeat(steps, shape[dim] // blocks).reshape([-1 if axis == dim else 1 for axis in range(len(shape))])
    return gain


def bell_draw(rng, dims, scale, limit, cuts=(), kind=jnp.bfloat16):
    level = levels(rng, dims, cuts, -0.22, 0.18) if cuts else 1.0
    entries = jax.random.normal(rng, dims, jnp.float32) * scale * level
    return jnp.minimum(jnp.maximum(entries, -limit), limit).astype(kind)


def setup_inputs(seed: int = 0) -> dict:
    seeds = jax.random.split(jax.random.key(seed), 6)
    return {
        "blocks": bell_draw(seeds[0], (RGROUPS, CGROUPS, NB_DEV, BQ, BD * BK), 1.0, 6.0, ((0, 8), (1, 4))),
        "coords": draw_coords(jax.random.fold_in(seeds[5], 71), 0),
        "counts": draw_counts(jax.random.fold_in(seeds[5], 71), 0),
        "doc_factor": bell_draw(seeds[3], (DOCS, R), 1.0, 6.0, ((0, 32),)),
        "ctx_factor": bell_draw(seeds[4], (CTX, R), (BD * BK) ** -0.5, 0.0625, ((0, 4),)),
    }


def reference(blocks, coords, counts, doc_factor, ctx_factor):
    total_slots = RGROUPS * CGROUPS * NB_DEV
    flat_blocks = blocks.reshape(total_slots, BQ, BD * BK)
    flat_coords = coords.reshape(total_slots, 3)

    def step(carry, index):
        group = index // NB_DEV
        slot = index % NB_DEV
        prow = group // CGROUPS
        pcol = group % CGROUPS
        place = flat_coords[index]
        valid = slot < counts[prow, pcol]
        qstart = ((prow * QB_ROW + place[0]) * BQ).astype(jnp.int32)
        dstart = ((pcol * DB_COL + place[1]) * BD).astype(jnp.int32)
        kstart = (place[2] * BK).astype(jnp.int32)
        brows = lax.dynamic_slice_in_dim(doc_factor, dstart, BD, 0).astype(jnp.float32)
        crows = lax.dynamic_slice_in_dim(ctx_factor, kstart, BK, 0).astype(jnp.float32)
        table = (brows[:, None, :] * crows[None, :, :]).reshape(BD * BK, R).astype(jnp.bfloat16)
        term = jnp.dot(flat_blocks[index], table, preferred_element_type=jnp.float32)
        term = jnp.where(valid, term, jnp.float32(0.0))
        current = lax.dynamic_slice_in_dim(carry, qstart, BQ, 0)
        carry = lax.dynamic_update_slice_in_dim(carry, current + term, qstart, 0)
        return carry, None

    start = jnp.zeros((QUERIES, R), jnp.float32)
    result, _ = lax.scan(step, start, jnp.arange(total_slots, dtype=jnp.int32))
    return result
```

```python
import functools

import jax
import jax.numpy as jnp
from jax import lax
from jax.experimental import pallas as pl
from jax.experimental.pallas import tpu as pltpu
from jax.sharding import PartitionSpec as P

BQ = 128
BD = 128
BK = 64
CHUNKS = 4
SEND = jnp.bfloat16
MESH = pl.DeviceIdType.MESH


def kernel(
    nrow, ncol, blocks, coords_hbm, counts_hbm, doc, ctx, out,
    coords, counts, xbuf, ctx_all, term, outbox, inbox,
    x_sem, own_sem, doc_send, doc_recv, sib_send, sib_recv, ctx_sem,
    ctx_send, ctx_recv, sum_send, sum_recv, *slabs,
):
    slots = xbuf.shape[0]
    nz = nrow // 2
    rows = BD // CHUNKS
    depth = rows * BK
    unit = ctx_all.shape[1]
    units = ctx.shape[0] // unit
    per_block = BK // unit
    me_r, me_c = lax.axis_index("row"), lax.axis_index("col")
    z, core = lax.div(me_r, 2), lax.rem(me_r, 2)
    sibling = z * 2 + (1 - core)

    def chip(j):
        return lax.rem(z + j + nz, nz) * 2 + core

    def column(j):
        return lax.rem(me_c + j + ncol, ncol)

    def load(h, s):
        return pltpu.make_async_copy(
            blocks.at[0, 0, s, :, pl.ds(h * depth, depth)],
            xbuf.at[s, :, pl.ds(h * depth, depth)],
            x_sem.at[h, s],
        )

    own_docs = [
        pltpu.make_async_copy(doc.at[pl.ds(h * rows, rows)], slabs[h].at[me_r], own_sem.at[2 + h])
        for h in range(CHUNKS)
    ]
    own_ctx = [
        pltpu.make_async_copy(
            ctx.at[pl.ds(i * unit, unit)], ctx_all.at[me_c * units + i], ctx_sem.at[i]
        )
        for i in range(units)
    ]
    own_coords = pltpu.make_async_copy(coords_hbm, coords, own_sem.at[0])
    own_counts = pltpu.make_async_copy(counts_hbm, counts, own_sem.at[1])
    own_coords.start()
    own_counts.start()
    for copy in own_docs + own_ctx:
        copy.start()
    for h in range(CHUNKS):
        for s in range(slots):
            load(h, s).start()

    barrier = pltpu.get_barrier_semaphore()
    peers = [(chip(j), me_c) for j in range(1, nz)] + [(sibling, me_c)]
    peers += [(me_r, column(j)) for j in range(1, ncol)]
    for peer in peers:
        pl.semaphore_signal(barrier, inc=1, device_id=peer, device_id_type=MESH)
    pl.semaphore_wait(barrier, len(peers))

    def send_ctx(j, i):
        return pltpu.make_async_remote_copy(
            src_ref=ctx.at[pl.ds(i * unit, unit)],
            dst_ref=ctx_all.at[me_c * units + i],
            send_sem=ctx_send.at[j, i], recv_sem=ctx_recv.at[j, i],
            device_id=(me_r, column(j)), device_id_type=MESH,
        )

    def slab_rows(row, h):
        return slabs[h].at[row]

    def send_doc(h, j):
        return pltpu.make_async_remote_copy(
            src_ref=doc.at[pl.ds(h * rows, rows)],
            dst_ref=slab_rows(me_r, h),
            send_sem=doc_send.at[h, j], recv_sem=doc_recv.at[h, j],
            device_id=(chip(j), me_c), device_id_type=MESH,
        )

    def send_sibling(h, j):
        return pltpu.make_async_remote_copy(
            src_ref=doc.at[pl.ds(h * rows, rows)] if j == 0 else slab_rows(chip(-j), h),
            dst_ref=slab_rows(me_r if j == 0 else chip(-j), h),
            send_sem=sib_send.at[h, j], recv_sem=sib_recv.at[h, j],
            device_id=(sibling, me_c), device_id_type=MESH,
        )

    for j in range(1, ncol):
        for i in range(units):
            send_ctx(j, i).start()
    for h in range(CHUNKS):
        for j in range(1, nz):
            send_doc(h, j).start()
        send_sibling(h, 0).start()

    def relay(h):
        for j in range(1, nz):
            send_doc(h, j).wait_recv()
            send_sibling(h, j).start()

    relay(0)
    own_coords.wait()
    own_counts.wait()
    for copy in own_docs + own_ctx:
        copy.wait()
    for j in range(1, ncol):
        for i in range(units):
            send_ctx(j, i).wait_recv()

    def multiply(h, s):
        load(h, s).wait()
        brows = slabs[h][coords[0, 1, 0, s]].astype(jnp.float32)
        first = coords[0, 2, 0, s] * per_block
        crows = jnp.concatenate([ctx_all[first + i] for i in range(per_block)], axis=0)
        crows = crows.reshape(BK // 16, 16, crows.shape[1])
        parts = []
        for b in range(rows):
            brow = jnp.broadcast_to(brows[b:b + 1, :], (16, brows.shape[1])).astype(jnp.bfloat16)
            parts.append((crows * brow[None]).reshape(BK, brows.shape[1]))
        table = jnp.concatenate(parts, axis=0)
        got = jnp.dot(
            xbuf[s, :, h * depth:(h + 1) * depth], table, preferred_element_type=jnp.float32
        )
        if h == 0:
            term[s] = got
        else:
            term[s] += got

    middle = (slots + 1) // 2
    for h in range(CHUNKS):
        for j in range(nz):
            send_sibling(h, j).wait_recv()

        def step(s, carry, h=h):
            multiply(h, s)
            return carry

        lax.fori_loop(0, middle, step, 0)
        if h + 1 < CHUNKS:
            relay(h + 1)
        lax.fori_loop(middle, slots, step, 0)

    used = counts[0, 0]

    def partial_sum(q):
        total = jnp.zeros(out.shape, jnp.float32)
        for s in range(slots):
            wanted = jnp.logical_and(
                jnp.full(out.shape, coords[0, 0, 0, s]) == q, jnp.full(out.shape, used) > s
            )
            total += jnp.where(wanted, term[s], 0.0)
        return total

    def send_sum(j):
        return pltpu.make_async_remote_copy(
            src_ref=outbox.at[j], dst_ref=inbox.at[j],
            send_sem=sum_send.at[j], recv_sem=sum_recv.at[j],
            device_id=(me_r, column(j)), device_id_type=MESH,
        )

    for j in range(1, ncol):
        outbox[j] = partial_sum(column(j)).astype(outbox.dtype)
        send_sum(j).start()
    total = partial_sum(me_c)
    for j in range(1, ncol):
        send_sum(j).wait_recv()
        total += inbox[j].astype(jnp.float32)
    out[...] = total

    for j in range(1, ncol):
        for i in range(units):
            send_ctx(j, i).wait_send()
        send_sum(j).wait_send()
    for h in range(CHUNKS):
        for j in range(1, nz):
            send_doc(h, j).wait_send()
        for j in range(nz):
            send_sibling(h, j).wait_send()


def body(nrow, ncol, blocks, coords, counts, doc_factor, ctx_factor):
    slots, width = blocks.shape[2], blocks.shape[4]
    rank = doc_factor.shape[1]
    nz = nrow // 2
    unit = min(BK, ctx_factor.shape[0])
    units = ctx_factor.shape[0] // unit
    dma = pltpu.SemaphoreType.DMA
    return pl.pallas_call(
        functools.partial(kernel, nrow, ncol),
        out_shape=jax.ShapeDtypeStruct((BQ, rank), jnp.float32),
        in_specs=[
            pl.BlockSpec(memory_space=pltpu.HBM),
            pl.BlockSpec(memory_space=pltpu.HBM),
            pl.BlockSpec(memory_space=pltpu.HBM),
            pl.BlockSpec(memory_space=pltpu.HBM),
            pl.BlockSpec(memory_space=pltpu.HBM),
        ],
        out_specs=pl.BlockSpec(memory_space=pltpu.VMEM),
        scratch_shapes=[
            pltpu.SMEM((1, 3, 1, slots), jnp.int32),
            pltpu.SMEM((1, 1), jnp.int32),
            pltpu.VMEM((slots, BQ, width), jnp.bfloat16),
            pltpu.VMEM((ctx_factor.shape[0] * ncol // unit, unit, rank), jnp.bfloat16),
            pltpu.VMEM((slots, BQ, rank), jnp.float32),
            pltpu.VMEM((ncol, BQ, rank), SEND),
            pltpu.VMEM((ncol, BQ, rank), SEND),
            dma((CHUNKS, slots)),
            dma((2 + CHUNKS,)),
            dma((CHUNKS, nz)),
            dma((CHUNKS, nz)),
            dma((CHUNKS, nz)),
            dma((CHUNKS, nz)),
            dma((units,)),
            dma((ncol, units)),
            dma((ncol, units)),
            dma((ncol,)),
            dma((ncol,)),
        ] + [pltpu.VMEM((nrow, BD // CHUNKS, rank), jnp.bfloat16)] * CHUNKS,
        compiler_params=pltpu.CompilerParams(
            collective_id=0, has_side_effects=True, vmem_limit_bytes=60 * 1024 * 1024
        ),
        cost_estimate=pl.CostEstimate(
            flops=2 * slots * BQ * width * rank,
            bytes_accessed=slots * BQ * width * 2,
            transcendentals=0,
        ),
    )(blocks, coords.transpose(0, 3, 1, 2), counts, doc_factor, ctx_factor)


def solution(mesh):
    placed = (
        P("row", "col", None, None, None),
        P("row", "col", None, None),
        P("row", "col"),
        P(("col", "row"), None),
        P("col", None),
    )
    return jax.shard_map(
        functools.partial(body, mesh.shape["row"], mesh.shape["col"]),
        mesh=mesh, in_specs=placed, out_specs=P(("row", "col"), None), check_vma=False,
    )
```

```python
import functools

import jax
import jax.numpy as jnp
from jax import lax
from jax.experimental import pallas as pl
from jax.experimental.pallas import tpu as pltpu
from jax.sharding import PartitionSpec as P

BQ = 128
BD = 128
BK = 64
CHUNKS = 2
SEND = jnp.bfloat16
MESH = pl.DeviceIdType.MESH


def kernel(
    nrow, ncol, blocks, coords_hbm, counts_hbm, doc, ctx, out,
    coords, counts, xbuf, ctx_all, term, outbox, inbox,
    x_sem, own_sem, doc_send, doc_recv, sib_send, sib_recv, ctx_sem,
    ctx_send, ctx_recv, sum_send, sum_recv, *slabs,
):
    slots = xbuf.shape[0]
    nz = nrow // 2
    rows = BD // CHUNKS
    depth = rows * BK
    unit = ctx_all.shape[1]
    units = ctx.shape[0] // unit
    per_block = BK // unit
    me_r, me_c = lax.axis_index("row"), lax.axis_index("col")
    z, core = lax.div(me_r, 2), lax.rem(me_r, 2)
    sibling = z * 2 + (1 - core)

    def chip(j):
        return lax.rem(z + j + nz, nz) * 2 + core

    def column(j):
        return lax.rem(me_c + j + ncol, ncol)

    def load(h, s):
        return pltpu.make_async_copy(
            blocks.at[0, 0, s, :, pl.ds(h * depth, depth)],
            xbuf.at[s, :, pl.ds(h * depth, depth)],
            x_sem.at[h, s],
        )

    barrier = pltpu.get_barrier_semaphore()
    peers = [(chip(j), me_c) for j in range(1, nz)] + [(sibling, me_c)]
    peers += [(me_r, column(j)) for j in range(1, ncol)]
    for peer in peers:
        pl.semaphore_signal(barrier, inc=1, device_id=peer, device_id_type=MESH)

    own_docs = [
        pltpu.make_async_copy(doc.at[pl.ds(h * rows, rows)], slabs[h].at[me_r], own_sem.at[2 + h])
        for h in range(CHUNKS)
    ]
    own_ctx = [
        pltpu.make_async_copy(
            ctx.at[pl.ds(i * unit, unit)], ctx_all.at[me_c * units + i], ctx_sem.at[i]
        )
        for i in range(units)
    ]
    own_coords = pltpu.make_async_copy(coords_hbm, coords, own_sem.at[0])
    own_counts = pltpu.make_async_copy(counts_hbm, counts, own_sem.at[1])
    own_coords.start()
    own_counts.start()
    for copy in own_docs + own_ctx:
        copy.start()
    for h in range(CHUNKS):
        for s in range(slots):
            load(h, s).start()

    pl.semaphore_wait(barrier, len(peers))

    def send_ctx(j, i):
        return pltpu.make_async_remote_copy(
            src_ref=ctx.at[pl.ds(i * unit, unit)],
            dst_ref=ctx_all.at[me_c * units + i],
            send_sem=ctx_send.at[j, i], recv_sem=ctx_recv.at[j, i],
            device_id=(me_r, column(j)), device_id_type=MESH,
        )

    def slab_rows(row, h):
        return slabs[h].at[row]

    def send_doc(h, j):
        return pltpu.make_async_remote_copy(
            src_ref=doc.at[pl.ds(h * rows, rows)],
            dst_ref=slab_rows(me_r, h),
            send_sem=doc_send.at[h, j], recv_sem=doc_recv.at[h, j],
            device_id=(chip(j), me_c), device_id_type=MESH,
        )

    def send_sibling(h, j):
        return pltpu.make_async_remote_copy(
            src_ref=doc.at[pl.ds(h * rows, rows)] if j == 0 else slab_rows(chip(-j), h),
            dst_ref=slab_rows(me_r if j == 0 else chip(-j), h),
            send_sem=sib_send.at[h, j], recv_sem=sib_recv.at[h, j],
            device_id=(sibling, me_c), device_id_type=MESH,
        )

    for j in range(1, ncol):
        for i in range(units):
            send_ctx(j, i).start()
    for h in range(CHUNKS):
        for j in range(1, nz):
            send_doc(h, j).start()
        send_sibling(h, 0).start()

    def relay(h):
        for j in range(1, nz):
            send_doc(h, j).wait_recv()
            send_sibling(h, j).start()

    relay(0)
    own_coords.wait()
    own_counts.wait()
    for copy in own_docs + own_ctx:
        copy.wait()
    for j in range(1, ncol):
        for i in range(units):
            send_ctx(j, i).wait_recv()

    def multiply(h, s):
        load(h, s).wait()
        brows = slabs[h][coords[0, 1, 0, s]].astype(jnp.float32)
        first = coords[0, 2, 0, s] * per_block
        crows = jnp.concatenate([ctx_all[first + i] for i in range(per_block)], axis=0)
        crows = crows.reshape(BK // 16, 16, crows.shape[1])
        parts = []
        for b in range(rows):
            brow = jnp.broadcast_to(brows[b:b + 1, :], (16, brows.shape[1])).astype(jnp.bfloat16)
            parts.append((crows * brow[None]).reshape(BK, brows.shape[1]))
        table = jnp.concatenate(parts, axis=0)
        got = jnp.dot(
            xbuf[s, :, h * depth:(h + 1) * depth], table, preferred_element_type=jnp.float32
        )
        if h == 0:
            term[s] = got
        else:
            term[s] += got

    middle = (slots + 1) // 2
    for h in range(CHUNKS):
        for j in range(nz):
            send_sibling(h, j).wait_recv()

        def step(s, carry, h=h):
            multiply(h, s)
            return carry

        if h + 1 < CHUNKS:
            lax.fori_loop(0, middle, step, 0)
            relay(h + 1)
            lax.fori_loop(middle, slots, step, 0)
        else:
            lax.fori_loop(0, slots, step, 0)

    used = counts[0, 0]

    def partial_sum(q):
        total = jnp.zeros(out.shape, jnp.float32)
        for s in range(slots):
            wanted = jnp.logical_and(
                jnp.full(out.shape, coords[0, 0, 0, s]) == q, jnp.full(out.shape, used) > s
            )
            total += jnp.where(wanted, term[s], 0.0)
        return total

    def send_sum(j):
        return pltpu.make_async_remote_copy(
            src_ref=outbox.at[j], dst_ref=inbox.at[j],
            send_sem=sum_send.at[j], recv_sem=sum_recv.at[j],
            device_id=(me_r, column(j)), device_id_type=MESH,
        )

    for j in range(1, ncol):
        outbox[j] = partial_sum(column(j)).astype(outbox.dtype)
        send_sum(j).start()
    total = partial_sum(me_c)
    for j in range(1, ncol):
        send_sum(j).wait_recv()
        total += inbox[j].astype(jnp.float32)
    out[...] = total

    for j in range(1, ncol):
        for i in range(units):
            send_ctx(j, i).wait_send()
        send_sum(j).wait_send()
    for h in range(CHUNKS):
        for j in range(1, nz):
            send_doc(h, j).wait_send()
        for j in range(nz):
            send_sibling(h, j).wait_send()


def body(nrow, ncol, blocks, coords, counts, doc_factor, ctx_factor):
    slots, width = blocks.shape[2], blocks.shape[4]
    rank = doc_factor.shape[1]
    nz = nrow // 2
    unit = min(BK, ctx_factor.shape[0])
    units = ctx_factor.shape[0] // unit
    dma = pltpu.SemaphoreType.DMA
    return pl.pallas_call(
        functools.partial(kernel, nrow, ncol),
        out_shape=jax.ShapeDtypeStruct((BQ, rank), jnp.float32),
        in_specs=[
            pl.BlockSpec(memory_space=pltpu.HBM),
            pl.BlockSpec(memory_space=pltpu.HBM),
            pl.BlockSpec(memory_space=pltpu.HBM),
            pl.BlockSpec(memory_space=pltpu.HBM),
            pl.BlockSpec(memory_space=pltpu.HBM),
        ],
        out_specs=pl.BlockSpec(memory_space=pltpu.VMEM),
        scratch_shapes=[
            pltpu.SMEM((1, 3, 1, slots), jnp.int32),
            pltpu.SMEM((1, 1), jnp.int32),
            pltpu.VMEM((slots, BQ, width), jnp.bfloat16),
            pltpu.VMEM((ctx_factor.shape[0] * ncol // unit, unit, rank), jnp.bfloat16),
            pltpu.VMEM((slots, BQ, rank), jnp.float32),
            pltpu.VMEM((ncol, BQ, rank), SEND),
            pltpu.VMEM((ncol, BQ, rank), SEND),
            dma((CHUNKS, slots)),
            dma((2 + CHUNKS,)),
            dma((CHUNKS, nz)),
            dma((CHUNKS, nz)),
            dma((CHUNKS, nz)),
            dma((CHUNKS, nz)),
            dma((units,)),
            dma((ncol, units)),
            dma((ncol, units)),
            dma((ncol,)),
            dma((ncol,)),
        ] + [pltpu.VMEM((nrow, BD // CHUNKS, rank), jnp.bfloat16)] * CHUNKS,
        compiler_params=pltpu.CompilerParams(
            collective_id=0, has_side_effects=True, vmem_limit_bytes=60 * 1024 * 1024
        ),
        cost_estimate=pl.CostEstimate(
            flops=2 * slots * BQ * width * rank,
            bytes_accessed=slots * BQ * width * 2,
            transcendentals=0,
        ),
    )(blocks, coords.transpose(0, 3, 1, 2), counts, doc_factor, ctx_factor)


def solution(mesh):
    placed = (
        P("row", "col", None, None, None),
        P("row", "col", None, None),
        P("row", "col"),
        P(("col", "row"), None),
        P("col", None),
    )
    return jax.shard_map(
        functools.partial(body, mesh.shape["row"], mesh.shape["col"]),
        mesh=mesh, in_specs=placed, out_specs=P(("row", "col"), None), check_vma=False,
    )
```

```python
import functools

import jax
import jax.numpy as jnp
from jax import lax
from jax.experimental import pallas as pl
from jax.experimental.pallas import tpu as pltpu
from jax.sharding import PartitionSpec as P

BQ = 128
BD = 128
BK = 64
CHUNKS = 2
SEND = jnp.bfloat16
MESH = pl.DeviceIdType.MESH


def kernel(
    nrow, ncol, blocks, coords_hbm, counts_hbm, doc, ctx, out,
    coords, counts, xbuf, ctx_all, term, outbox, inbox,
    x_sem, own_sem, doc_send, doc_recv, sib_send, sib_recv, ctx_sem,
    ctx_send, ctx_recv, sum_send, sum_recv, *slabs,
):
    slots = xbuf.shape[0]
    nz = nrow // 2
    rows = BD // CHUNKS
    depth = rows * BK
    unit = ctx_all.shape[1]
    units = ctx.shape[0] // unit
    per_block = BK // unit
    me_r, me_c = lax.axis_index("row"), lax.axis_index("col")
    z, core = lax.div(me_r, 2), lax.rem(me_r, 2)
    sibling = z * 2 + (1 - core)

    def chip(j):
        return lax.rem(z + j + nz, nz) * 2 + core

    def column(j):
        return lax.rem(me_c + j + ncol, ncol)

    def load(h, s):
        return pltpu.make_async_copy(
            blocks.at[0, 0, s, :, pl.ds(h * depth, depth)],
            xbuf.at[s, :, pl.ds(h * depth, depth)],
            x_sem.at[h, s],
        )

    barrier = pltpu.get_barrier_semaphore()
    peers = [(chip(j), me_c) for j in range(1, nz)] + [(sibling, me_c)]
    peers += [(me_r, column(j)) for j in range(1, ncol)]
    for peer in peers:
        pl.semaphore_signal(barrier, inc=1, device_id=peer, device_id_type=MESH)

    own_docs = [
        pltpu.make_async_copy(doc.at[pl.ds(h * rows, rows)], slabs[h].at[me_r], own_sem.at[2 + h])
        for h in range(CHUNKS)
    ]
    own_ctx = [
        pltpu.make_async_copy(
            ctx.at[pl.ds(i * unit, unit)], ctx_all.at[me_c * units + i], ctx_sem.at[i]
        )
        for i in range(units)
    ]
    own_coords = pltpu.make_async_copy(coords_hbm, coords, own_sem.at[0])
    own_counts = pltpu.make_async_copy(counts_hbm, counts, own_sem.at[1])
    own_coords.start()
    own_counts.start()
    for copy in own_docs + own_ctx:
        copy.start()
    for h in range(CHUNKS):
        for s in range(slots):
            load(h, s).start()

    pl.semaphore_wait(barrier, len(peers))

    def send_ctx(j, i):
        return pltpu.make_async_remote_copy(
            src_ref=ctx.at[pl.ds(i * unit, unit)],
            dst_ref=ctx_all.at[me_c * units + i],
            send_sem=ctx_send.at[j, i], recv_sem=ctx_recv.at[j, i],
            device_id=(me_r, column(j)), device_id_type=MESH,
        )

    def slab_rows(row, h):
        return slabs[h].at[row]

    def send_doc(h, j):
        return pltpu.make_async_remote_copy(
            src_ref=doc.at[pl.ds(h * rows, rows)],
            dst_ref=slab_rows(me_r, h),
            send_sem=doc_send.at[h, j], recv_sem=doc_recv.at[h, j],
            device_id=(chip(j), me_c), device_id_type=MESH,
        )

    def send_sibling(h, j):
        return pltpu.make_async_remote_copy(
            src_ref=doc.at[pl.ds(h * rows, rows)] if j == 0 else slab_rows(chip(-j), h),
            dst_ref=slab_rows(me_r if j == 0 else chip(-j), h),
            send_sem=sib_send.at[h, j], recv_sem=sib_recv.at[h, j],
            device_id=(sibling, me_c), device_id_type=MESH,
        )

    for j in range(1, ncol):
        for i in range(units):
            send_ctx(j, i).start()
    for h in range(CHUNKS):
        for j in range(1, nz):
            send_doc(h, j).start()
        send_sibling(h, 0).start()

    def relay(h):
        for j in range(1, nz):
            send_doc(h, j).wait_recv()
            send_sibling(h, j).start()

    relay(0)
    own_coords.wait()
    own_counts.wait()
    for copy in own_docs + own_ctx:
        copy.wait()
    for j in range(1, ncol):
        for i in range(units):
            send_ctx(j, i).wait_recv()

    def multiply(h, s):
        load(h, s).wait()
        brows = slabs[h][coords[0, 1, 0, s]].astype(jnp.float32)
        first = coords[0, 2, 0, s] * per_block
        crows = jnp.concatenate([ctx_all[first + i] for i in range(per_block)], axis=0)
        crows = crows.reshape(BK // 16, 16, crows.shape[1])
        parts = []
        for b in range(rows):
            brow = jnp.broadcast_to(brows[b:b + 1, :], (16, brows.shape[1])).astype(jnp.bfloat16)
            parts.append((crows * brow[None]).reshape(BK, brows.shape[1]))
        half = depth // 2
        table = jnp.concatenate(
            [jnp.concatenate(parts[:rows // 2], axis=0), jnp.concatenate(parts[rows // 2:], axis=0)],
            axis=1,
        )
        left = jnp.concatenate(
            [
                xbuf[s, :, h * depth:h * depth + half],
                xbuf[s, :, h * depth + half:(h + 1) * depth],
            ],
            axis=0,
        )
        both = jnp.dot(left, table, preferred_element_type=jnp.float32)
        got = both[:BQ, :brows.shape[1]] + both[BQ:, brows.shape[1]:]
        if h == 0:
            term[s] = got
        else:
            term[s] += got

    middle = (slots + 1) // 2
    for h in range(CHUNKS):
        for j in range(nz):
            send_sibling(h, j).wait_recv()

        def step(s, carry, h=h):
            multiply(h, s)
            return carry

        if h + 1 < CHUNKS:
            lax.fori_loop(0, middle, step, 0)
            relay(h + 1)
            lax.fori_loop(middle, slots, step, 0)
        else:
            lax.fori_loop(0, slots, step, 0)

    used = counts[0, 0]

    def partial_sum(q):
        total = jnp.zeros(out.shape, jnp.float32)
        for s in range(slots):
            wanted = jnp.logical_and(
                jnp.full(out.shape, coords[0, 0, 0, s]) == q, jnp.full(out.shape, used) > s
            )
            total += jnp.where(wanted, term[s], 0.0)
        return total

    def send_sum(j):
        return pltpu.make_async_remote_copy(
            src_ref=outbox.at[j], dst_ref=inbox.at[j],
            send_sem=sum_send.at[j], recv_sem=sum_recv.at[j],
            device_id=(me_r, column(j)), device_id_type=MESH,
        )

    for j in range(1, ncol):
        outbox[j] = partial_sum(column(j)).astype(outbox.dtype)
        send_sum(j).start()
    total = partial_sum(me_c)
    for j in range(1, ncol):
        send_sum(j).wait_recv()
        total += inbox[j].astype(jnp.float32)
    out[...] = total

    for j in range(1, ncol):
        for i in range(units):
            send_ctx(j, i).wait_send()
        send_sum(j).wait_send()
    for h in range(CHUNKS):
        for j in range(1, nz):
            send_doc(h, j).wait_send()
        for j in range(nz):
            send_sibling(h, j).wait_send()


def body(nrow, ncol, blocks, coords, counts, doc_factor, ctx_factor):
    slots, width = blocks.shape[2], blocks.shape[4]
    rank = doc_factor.shape[1]
    nz = nrow // 2
    unit = min(BK, ctx_factor.shape[0])
    units = ctx_factor.shape[0] // unit
    dma = pltpu.SemaphoreType.DMA
    return pl.pallas_call(
        functools.partial(kernel, nrow, ncol),
        out_shape=jax.ShapeDtypeStruct((BQ, rank), jnp.float32),
        in_specs=[
            pl.BlockSpec(memory_space=pltpu.HBM),
            pl.BlockSpec(memory_space=pltpu.HBM),
            pl.BlockSpec(memory_space=pltpu.HBM),
            pl.BlockSpec(memory_space=pltpu.HBM),
            pl.BlockSpec(memory_space=pltpu.HBM),
        ],
        out_specs=pl.BlockSpec(memory_space=pltpu.VMEM),
        scratch_shapes=[
            pltpu.SMEM((1, 3, 1, slots), jnp.int32),
            pltpu.SMEM((1, 1), jnp.int32),
            pltpu.VMEM((slots, BQ, width), jnp.bfloat16),
            pltpu.VMEM((ctx_factor.shape[0] * ncol // unit, unit, rank), jnp.bfloat16),
            pltpu.VMEM((slots, BQ, rank), jnp.float32),
            pltpu.VMEM((ncol, BQ, rank), SEND),
            pltpu.VMEM((ncol, BQ, rank), SEND),
            dma((CHUNKS, slots)),
            dma((2 + CHUNKS,)),
            dma((CHUNKS, nz)),
            dma((CHUNKS, nz)),
            dma((CHUNKS, nz)),
            dma((CHUNKS, nz)),
            dma((units,)),
            dma((ncol, units)),
            dma((ncol, units)),
            dma((ncol,)),
            dma((ncol,)),
        ] + [pltpu.VMEM((nrow, BD // CHUNKS, rank), jnp.bfloat16)] * CHUNKS,
        compiler_params=pltpu.CompilerParams(
            collective_id=0, has_side_effects=True, vmem_limit_bytes=60 * 1024 * 1024
        ),
        cost_estimate=pl.CostEstimate(
            flops=2 * slots * BQ * width * rank,
            bytes_accessed=slots * BQ * width * 2,
            transcendentals=0,
        ),
    )(blocks, coords.transpose(0, 3, 1, 2), counts, doc_factor, ctx_factor)


def solution(mesh):
    placed = (
        P("row", "col", None, None, None),
        P("row", "col", None, None),
        P("row", "col"),
        P(("col", "row"), None),
        P("col", None),
    )
    return jax.shard_map(
        functools.partial(body, mesh.shape["row"], mesh.shape["col"]),
        mesh=mesh, in_specs=placed, out_specs=P(("row", "col"), None), check_vma=False,
    )
```

```python
import functools

import jax
import jax.numpy as jnp
from jax import lax
from jax.experimental import pallas as pl
from jax.experimental.pallas import tpu as pltpu
from jax.sharding import PartitionSpec as P

BQ = 128
BD = 128
BK = 64
CHUNKS = 2
PIECE = 8
SEND = jnp.bfloat16
MESH = pl.DeviceIdType.MESH


def kernel(
    nrow, ncol, blocks, coords_hbm, counts_hbm, doc, ctx, out, inbox,
    coords, counts, xbuf, ctx_all, term, outbox, own,
    x_sem, own_sem, doc_send, doc_recv, sib_send, sib_recv, ctx_sem,
    ctx_send, ctx_recv, sum_send, sum_recv, *slabs,
):
    slots = xbuf.shape[0]
    nz = nrow // 2
    rows = BD // CHUNKS
    depth = rows * BK
    unit = ctx_all.shape[1]
    units = ctx.shape[0] // unit
    per_block = BK // unit
    me_r, me_c = lax.axis_index("row"), lax.axis_index("col")
    z, core = lax.div(me_r, 2), lax.rem(me_r, 2)
    sibling = z * 2 + (1 - core)

    def chip(j):
        return lax.rem(z + j + nz, nz) * 2 + core

    def column(j):
        return lax.rem(me_c + j + ncol, ncol)

    def load(h, s):
        return pltpu.make_async_copy(
            blocks.at[0, 0, s, :, pl.ds(h * depth, depth)],
            xbuf.at[s, :, pl.ds(h * depth, depth)],
            x_sem.at[h, s],
        )

    barrier = pltpu.get_barrier_semaphore()
    peers = [(chip(j), me_c) for j in range(1, nz)] + [(sibling, me_c)]
    peers += [(me_r, column(j)) for j in range(1, ncol)]
    for peer in peers:
        pl.semaphore_signal(barrier, inc=1, device_id=peer, device_id_type=MESH)

    own_docs = [
        pltpu.make_async_copy(doc.at[pl.ds(h * rows, rows)], slabs[h].at[me_r], own_sem.at[2 + h])
        for h in range(CHUNKS)
    ]
    own_ctx = [
        pltpu.make_async_copy(
            ctx.at[pl.ds(i * unit, unit)], ctx_all.at[me_c * units + i], ctx_sem.at[i]
        )
        for i in range(units)
    ]
    own_coords = pltpu.make_async_copy(coords_hbm, coords, own_sem.at[0])
    own_counts = pltpu.make_async_copy(counts_hbm, counts, own_sem.at[1])
    own_coords.start()
    own_counts.start()
    for copy in own_docs + own_ctx:
        copy.start()
    for h in range(CHUNKS):
        for s in range(slots):
            load(h, s).start()

    pl.semaphore_wait(barrier, len(peers))

    def send_ctx(j, i):
        return pltpu.make_async_remote_copy(
            src_ref=ctx.at[pl.ds(i * unit, unit)],
            dst_ref=ctx_all.at[me_c * units + i],
            send_sem=ctx_send.at[j, i], recv_sem=ctx_recv.at[j, i],
            device_id=(me_r, column(j)), device_id_type=MESH,
        )

    def slab_rows(row, h):
        return slabs[h].at[row]

    def send_doc(h, j):
        return pltpu.make_async_remote_copy(
            src_ref=doc.at[pl.ds(h * rows, rows)],
            dst_ref=slab_rows(me_r, h),
            send_sem=doc_send.at[h, j], recv_sem=doc_recv.at[h, j],
            device_id=(chip(j), me_c), device_id_type=MESH,
        )

    def send_sibling(h, j):
        return pltpu.make_async_remote_copy(
            src_ref=doc.at[pl.ds(h * rows, rows)] if j == 0 else slab_rows(chip(-j), h),
            dst_ref=slab_rows(me_r if j == 0 else chip(-j), h),
            send_sem=sib_send.at[h, j], recv_sem=sib_recv.at[h, j],
            device_id=(sibling, me_c), device_id_type=MESH,
        )

    for j in range(1, ncol):
        for i in range(units):
            send_ctx(j, i).start()
    for h in range(CHUNKS):
        for j in range(1, nz):
            send_doc(h, j).start()
        send_sibling(h, 0).start()

    def relay(h):
        for j in range(1, nz):
            send_doc(h, j).wait_recv()
            send_sibling(h, j).start()

    relay(0)
    own_coords.wait()
    own_counts.wait()
    for copy in own_docs + own_ctx:
        copy.wait()
    for j in range(1, ncol):
        for i in range(units):
            send_ctx(j, i).wait_recv()

    def multiply(h, s):
        load(h, s).wait()
        brows = slabs[h][coords[0, 1, 0, s]].astype(jnp.float32)
        first = coords[0, 2, 0, s] * per_block
        crows = jnp.concatenate([ctx_all[first + i] for i in range(per_block)], axis=0)
        crows = crows.reshape(BK // 16, 16, crows.shape[1])
        got = None
        for b in range(0, rows, PIECE):
            parts = []
            for i in range(b, b + PIECE):
                brow = jnp.broadcast_to(brows[i:i + 1, :], (16, brows.shape[1]))
                parts.append((crows * brow.astype(jnp.bfloat16)[None]).reshape(BK, brows.shape[1]))
            piece = jnp.dot(
                xbuf[s, :, h * depth + b * BK:h * depth + (b + PIECE) * BK],
                jnp.concatenate(parts, axis=0), preferred_element_type=jnp.float32,
            )
            got = piece if got is None else got + piece
        if h == 0:
            term[s] = got
        else:
            term[s] += got

    middle = (slots + 1) // 2
    for h in range(CHUNKS):
        for j in range(nz):
            send_sibling(h, j).wait_recv()

        def step(s, carry, h=h):
            multiply(h, s)
            return carry

        if h + 1 < CHUNKS:
            lax.fori_loop(0, middle, step, 0)
            relay(h + 1)
            lax.fori_loop(middle, slots, step, 0)
        else:
            lax.fori_loop(0, slots, step, 0)

    used = counts[0, 0]

    def partial_sum(q):
        total = jnp.zeros(own.shape, jnp.float32)
        for s in range(slots):
            wanted = jnp.logical_and(
                jnp.full(own.shape, coords[0, 0, 0, s]) == q, jnp.full(own.shape, used) > s
            )
            total += jnp.where(wanted, term[s], 0.0)
        return total

    def send_sum(j):
        return pltpu.make_async_remote_copy(
            src_ref=outbox.at[j], dst_ref=inbox.at[j - 1],
            send_sem=sum_send.at[j], recv_sem=sum_recv.at[j],
            device_id=(me_r, column(j)), device_id_type=MESH,
        )

    for j in range(1, ncol):
        outbox[j] = partial_sum(column(j)).astype(outbox.dtype)
        send_sum(j).start()
    own[...] = partial_sum(me_c)
    result = pltpu.make_async_copy(own, out, own_sem.at[0])
    result.start()
    for j in range(1, ncol):
        send_sum(j).wait_recv()
    result.wait()

    for j in range(1, ncol):
        for i in range(units):
            send_ctx(j, i).wait_send()
        send_sum(j).wait_send()
    for h in range(CHUNKS):
        for j in range(1, nz):
            send_doc(h, j).wait_send()
        for j in range(nz):
            send_sibling(h, j).wait_send()


def body(nrow, ncol, blocks, coords, counts, doc_factor, ctx_factor):
    slots, width = blocks.shape[2], blocks.shape[4]
    rank = doc_factor.shape[1]
    nz = nrow // 2
    unit = min(BK, ctx_factor.shape[0])
    units = ctx_factor.shape[0] // unit
    dma = pltpu.SemaphoreType.DMA
    own, inbox = pl.pallas_call(
        functools.partial(kernel, nrow, ncol),
        out_shape=(
            jax.ShapeDtypeStruct((BQ, rank), jnp.float32),
            jax.ShapeDtypeStruct((ncol - 1, BQ, rank), SEND),
        ),
        in_specs=[
            pl.BlockSpec(memory_space=pltpu.HBM),
            pl.BlockSpec(memory_space=pltpu.HBM),
            pl.BlockSpec(memory_space=pltpu.HBM),
            pl.BlockSpec(memory_space=pltpu.HBM),
            pl.BlockSpec(memory_space=pltpu.HBM),
        ],
        out_specs=(
            pl.BlockSpec(memory_space=pltpu.HBM),
            pl.BlockSpec(memory_space=pltpu.HBM),
        ),
        scratch_shapes=[
            pltpu.SMEM((1, 3, 1, slots), jnp.int32),
            pltpu.SMEM((1, 1), jnp.int32),
            pltpu.VMEM((slots, BQ, width), jnp.bfloat16),
            pltpu.VMEM((ctx_factor.shape[0] * ncol // unit, unit, rank), jnp.bfloat16),
            pltpu.VMEM((slots, BQ, rank), jnp.float32),
            pltpu.VMEM((ncol, BQ, rank), SEND),
            pltpu.VMEM((BQ, rank), jnp.float32),
            dma((CHUNKS, slots)),
            dma((2 + CHUNKS,)),
            dma((CHUNKS, nz)),
            dma((CHUNKS, nz)),
            dma((CHUNKS, nz)),
            dma((CHUNKS, nz)),
            dma((units,)),
            dma((ncol, units)),
            dma((ncol, units)),
            dma((ncol,)),
            dma((ncol,)),
        ] + [pltpu.VMEM((nrow, BD // CHUNKS, rank), jnp.bfloat16)] * CHUNKS,
        compiler_params=pltpu.CompilerParams(
            collective_id=0, has_side_effects=True, vmem_limit_bytes=60 * 1024 * 1024
        ),
        cost_estimate=pl.CostEstimate(
            flops=2 * slots * BQ * width * rank,
            bytes_accessed=slots * BQ * width * 2,
            transcendentals=0,
        ),
    )(blocks, coords.transpose(0, 3, 1, 2), counts, doc_factor, ctx_factor)
    return own + jnp.sum(inbox.astype(jnp.float32), axis=0)


def solution(mesh):
    placed = (
        P("row", "col", None, None, None),
        P("row", "col", None, None),
        P("row", "col"),
        P(("col", "row"), None),
        P("col", None),
    )
    return jax.shard_map(
        functools.partial(body, mesh.shape["row"], mesh.shape["col"]),
        mesh=mesh, in_specs=placed, out_specs=P(("row", "col"), None), check_vma=False,
    )
```

```python
import functools

import jax
import jax.numpy as jnp
from jax import lax
from jax.experimental import pallas as pl
from jax.experimental.pallas import tpu as pltpu
from jax.sharding import PartitionSpec as P

BQ = 128
BD = 128
BK = 64
CHUNKS = 2
PIECE = 8
SEND = jnp.bfloat16
MESH = pl.DeviceIdType.MESH


def kernel(
    nrow, ncol, blocks, coords_hbm, counts_hbm, doc, ctx, out, inbox,
    coords, counts, xbuf, ctx_all, term, outbox, own,
    x_sem, own_sem, doc_send, doc_recv, sib_send, sib_recv, ctx_sem,
    ctx_send, ctx_recv, sum_send, sum_recv, *slabs,
):
    slots = xbuf.shape[0]
    nz = nrow // 2
    rows = BD // CHUNKS
    depth = rows * BK
    unit = ctx_all.shape[1]
    units = ctx.shape[0] // unit
    per_block = BK // unit
    me_r, me_c = lax.axis_index("row"), lax.axis_index("col")
    z, core = lax.div(me_r, 2), lax.rem(me_r, 2)
    sibling = z * 2 + (1 - core)

    def chip(j):
        return lax.rem(z + j + nz, nz) * 2 + core

    def column(j):
        return lax.rem(me_c + j + ncol, ncol)

    def load(h, s):
        return pltpu.make_async_copy(
            blocks.at[0, 0, s, :, pl.ds(h * depth, depth)],
            xbuf.at[s, :, pl.ds(h * depth, depth)],
            x_sem.at[h, s],
        )

    barrier = pltpu.get_barrier_semaphore()
    peers = [(chip(j), me_c) for j in range(1, nz)] + [(sibling, me_c)]
    peers += [(me_r, column(j)) for j in range(1, ncol)]
    for peer in peers:
        pl.semaphore_signal(barrier, inc=1, device_id=peer, device_id_type=MESH)

    own_docs = [
        pltpu.make_async_copy(doc.at[pl.ds(h * rows, rows)], slabs[h].at[me_r], own_sem.at[2 + h])
        for h in range(CHUNKS)
    ]
    own_ctx = [
        pltpu.make_async_copy(
            ctx.at[pl.ds(i * unit, unit)], ctx_all.at[me_c * units + i], ctx_sem.at[i]
        )
        for i in range(units)
    ]
    own_coords = pltpu.make_async_copy(coords_hbm, coords, own_sem.at[0])
    own_counts = pltpu.make_async_copy(counts_hbm, counts, own_sem.at[1])
    own_coords.start()
    own_counts.start()
    for copy in own_docs + own_ctx:
        copy.start()
    for s in range(slots):
        load(0, s).start()

    pl.semaphore_wait(barrier, len(peers))

    def send_ctx(j, i):
        return pltpu.make_async_remote_copy(
            src_ref=ctx.at[pl.ds(i * unit, unit)],
            dst_ref=ctx_all.at[me_c * units + i],
            send_sem=ctx_send.at[j, i], recv_sem=ctx_recv.at[j, i],
            device_id=(me_r, column(j)), device_id_type=MESH,
        )

    def slab_rows(row, h):
        return slabs[h].at[row]

    def send_doc(h, j):
        return pltpu.make_async_remote_copy(
            src_ref=doc.at[pl.ds(h * rows, rows)],
            dst_ref=slab_rows(me_r, h),
            send_sem=doc_send.at[h, j], recv_sem=doc_recv.at[h, j],
            device_id=(chip(j), me_c), device_id_type=MESH,
        )

    def send_sibling(h, j):
        return pltpu.make_async_remote_copy(
            src_ref=doc.at[pl.ds(h * rows, rows)] if j == 0 else slab_rows(chip(-j), h),
            dst_ref=slab_rows(me_r if j == 0 else chip(-j), h),
            send_sem=sib_send.at[h, j], recv_sem=sib_recv.at[h, j],
            device_id=(sibling, me_c), device_id_type=MESH,
        )

    for j in range(1, ncol):
        for i in range(units):
            send_ctx(j, i).start()
    for h in range(CHUNKS):
        for j in range(1, nz):
            send_doc(h, j).start()
        send_sibling(h, 0).start()

    def relay(h):
        for j in range(1, nz):
            send_doc(h, j).wait_recv()
            send_sibling(h, j).start()

    relay(0)
    for h in range(1, CHUNKS):
        for s in range(slots):
            load(h, s).start()
    own_coords.wait()
    own_counts.wait()
    for copy in own_docs + own_ctx:
        copy.wait()
    for j in range(1, ncol):
        for i in range(units):
            send_ctx(j, i).wait_recv()

    def multiply(h, s):
        load(h, s).wait()
        brows = slabs[h][coords[0, 1, 0, s]].astype(jnp.float32)
        first = coords[0, 2, 0, s] * per_block
        crows = jnp.concatenate([ctx_all[first + i] for i in range(per_block)], axis=0)
        crows = crows.reshape(BK // 16, 16, crows.shape[1])
        got = None
        for b in range(0, rows, PIECE):
            parts = []
            for i in range(b, b + PIECE):
                brow = jnp.broadcast_to(brows[i:i + 1, :], (16, brows.shape[1]))
                parts.append((crows * brow.astype(jnp.bfloat16)[None]).reshape(BK, brows.shape[1]))
            piece = jnp.dot(
                xbuf[s, :, h * depth + b * BK:h * depth + (b + PIECE) * BK],
                jnp.concatenate(parts, axis=0), preferred_element_type=jnp.float32,
            )
            got = piece if got is None else got + piece
        if h == 0:
            term[s] = got
        else:
            term[s] += got

    middle = (slots + 1) // 2
    for h in range(CHUNKS):
        for j in range(nz):
            send_sibling(h, j).wait_recv()

        def step(s, carry, h=h):
            multiply(h, s)
            return carry

        if h + 1 < CHUNKS:
            lax.fori_loop(0, middle, step, 0)
            relay(h + 1)
            lax.fori_loop(middle, slots, step, 0)
        else:
            lax.fori_loop(0, slots, step, 0)

    used = counts[0, 0]

    def partial_sum(q):
        total = jnp.zeros(own.shape, jnp.float32)
        for s in range(slots):
            wanted = jnp.logical_and(
                jnp.full(own.shape, coords[0, 0, 0, s]) == q, jnp.full(own.shape, used) > s
            )
            total += jnp.where(wanted, term[s], 0.0)
        return total

    def send_sum(j):
        return pltpu.make_async_remote_copy(
            src_ref=outbox.at[j], dst_ref=inbox.at[j - 1],
            send_sem=sum_send.at[j], recv_sem=sum_recv.at[j],
            device_id=(me_r, column(j)), device_id_type=MESH,
        )

    for j in range(1, ncol):
        outbox[j] = partial_sum(column(j)).astype(outbox.dtype)
        send_sum(j).start()
    own[...] = partial_sum(me_c)
    result = pltpu.make_async_copy(own, out, own_sem.at[0])
    result.start()
    for j in range(1, ncol):
        send_sum(j).wait_recv()
    result.wait()

    for j in range(1, ncol):
        for i in range(units):
            send_ctx(j, i).wait_send()
        send_sum(j).wait_send()
    for h in range(CHUNKS):
        for j in range(1, nz):
            send_doc(h, j).wait_send()
        for j in range(nz):
            send_sibling(h, j).wait_send()


def body(nrow, ncol, blocks, coords, counts, doc_factor, ctx_factor):
    slots, width = blocks.shape[2], blocks.shape[4]
    rank = doc_factor.shape[1]
    nz = nrow // 2
    unit = min(BK, ctx_factor.shape[0])
    units = ctx_factor.shape[0] // unit
    dma = pltpu.SemaphoreType.DMA
    own, inbox = pl.pallas_call(
        functools.partial(kernel, nrow, ncol),
        out_shape=(
            jax.ShapeDtypeStruct((BQ, rank), jnp.float32),
            jax.ShapeDtypeStruct((ncol - 1, BQ, rank), SEND),
        ),
        in_specs=[
            pl.BlockSpec(memory_space=pltpu.HBM),
            pl.BlockSpec(memory_space=pltpu.HBM),
            pl.BlockSpec(memory_space=pltpu.HBM),
            pl.BlockSpec(memory_space=pltpu.HBM),
            pl.BlockSpec(memory_space=pltpu.HBM),
        ],
        out_specs=(
            pl.BlockSpec(memory_space=pltpu.HBM),
            pl.BlockSpec(memory_space=pltpu.HBM),
        ),
        scratch_shapes=[
            pltpu.SMEM((1, 3, 1, slots), jnp.int32),
            pltpu.SMEM((1, 1), jnp.int32),
            pltpu.VMEM((slots, BQ, width), jnp.bfloat16),
            pltpu.VMEM((ctx_factor.shape[0] * ncol // unit, unit, rank), jnp.bfloat16),
            pltpu.VMEM((slots, BQ, rank), jnp.float32),
            pltpu.VMEM((ncol, BQ, rank), SEND),
            pltpu.VMEM((BQ, rank), jnp.float32),
            dma((CHUNKS, slots)),
            dma((2 + CHUNKS,)),
            dma((CHUNKS, nz)),
            dma((CHUNKS, nz)),
            dma((CHUNKS, nz)),
            dma((CHUNKS, nz)),
            dma((units,)),
            dma((ncol, units)),
            dma((ncol, units)),
            dma((ncol,)),
            dma((ncol,)),
        ] + [pltpu.VMEM((nrow, BD // CHUNKS, rank), jnp.bfloat16)] * CHUNKS,
        compiler_params=pltpu.CompilerParams(
            collective_id=0, has_side_effects=True, vmem_limit_bytes=60 * 1024 * 1024
        ),
        cost_estimate=pl.CostEstimate(
            flops=2 * slots * BQ * width * rank,
            bytes_accessed=slots * BQ * width * 2,
            transcendentals=0,
        ),
    )(blocks, coords.transpose(0, 3, 1, 2), counts, doc_factor, ctx_factor)
    for j in range(ncol - 1):
        own = own + inbox[j].astype(jnp.float32)
    return own


def solution(mesh):
    placed = (
        P("row", "col", None, None, None),
        P("row", "col", None, None),
        P("row", "col"),
        P(("col", "row"), None),
        P("col", None),
    )
    return jax.shard_map(
        functools.partial(body, mesh.shape["row"], mesh.shape["col"]),
        mesh=mesh, in_specs=placed, out_specs=P(("row", "col"), None), check_vma=False,
    )
```

```python
import functools

import jax
import jax.numpy as jnp
from jax import lax
from jax.experimental import pallas as pl
from jax.experimental.pallas import tpu as pltpu
from jax.sharding import PartitionSpec as P

BQ = 128
BD = 128
BK = 64
CHUNKS = 2
PIECE = 8
SEND = jnp.bfloat16
MESH = pl.DeviceIdType.MESH


def kernel(
    nrow, ncol, blocks, coords_hbm, counts_hbm, doc, ctx, out, inbox,
    coords, counts, xbuf, ctx_all, term, outbox, own,
    x_sem, own_sem, doc_send, doc_recv, sib_send, sib_recv, ctx_sem,
    ctx_send, ctx_recv, sum_send, sum_recv, *slabs,
):
    slots = xbuf.shape[0]
    nz = nrow // 2
    rows = BD // CHUNKS
    depth = rows * BK
    unit = ctx_all.shape[1]
    units = ctx.shape[0] // unit
    per_block = BK // unit
    me_r, me_c = lax.axis_index("row"), lax.axis_index("col")
    z, core = lax.div(me_r, 2), lax.rem(me_r, 2)
    sibling = z * 2 + (1 - core)

    def chip(j):
        return lax.rem(z + j + nz, nz) * 2 + core

    def column(j):
        return lax.rem(me_c + j + ncol, ncol)

    def load(h, s):
        return pltpu.make_async_copy(
            blocks.at[0, 0, s, :, pl.ds(h * depth, depth)],
            xbuf.at[s, :, pl.ds(h * depth, depth)],
            x_sem.at[h, s],
        )

    barrier = pltpu.get_barrier_semaphore()
    peers = [(chip(j), me_c) for j in range(1, nz)] + [(sibling, me_c)]
    peers += [(me_r, column(j)) for j in range(1, ncol)]
    for peer in peers:
        pl.semaphore_signal(barrier, inc=1, device_id=peer, device_id_type=MESH)

    own_docs = [
        pltpu.make_async_copy(doc.at[pl.ds(h * rows, rows)], slabs[h].at[me_r], own_sem.at[2 + h])
        for h in range(CHUNKS)
    ]
    own_ctx = [
        pltpu.make_async_copy(
            ctx.at[pl.ds(i * unit, unit)], ctx_all.at[me_c * units + i], ctx_sem.at[i]
        )
        for i in range(units)
    ]
    own_coords = pltpu.make_async_copy(coords_hbm, coords, own_sem.at[0])
    own_counts = pltpu.make_async_copy(counts_hbm, counts, own_sem.at[1])
    own_coords.start()
    own_counts.start()
    for copy in own_docs + own_ctx:
        copy.start()
    for s in range(slots):
        load(0, s).start()

    pl.semaphore_wait(barrier, len(peers))

    def send_ctx(j, i):
        return pltpu.make_async_remote_copy(
            src_ref=ctx.at[pl.ds(i * unit, unit)],
            dst_ref=ctx_all.at[me_c * units + i],
            send_sem=ctx_send.at[j, i], recv_sem=ctx_recv.at[j, i],
            device_id=(me_r, column(j)), device_id_type=MESH,
        )

    def slab_rows(row, h):
        return slabs[h].at[row]

    def send_doc(h, j):
        return pltpu.make_async_remote_copy(
            src_ref=doc.at[pl.ds(h * rows, rows)],
            dst_ref=slab_rows(me_r, h),
            send_sem=doc_send.at[h, j], recv_sem=doc_recv.at[h, j],
            device_id=(chip(j), me_c), device_id_type=MESH,
        )

    def send_sibling(h, j):
        return pltpu.make_async_remote_copy(
            src_ref=doc.at[pl.ds(h * rows, rows)] if j == 0 else slab_rows(chip(-j), h),
            dst_ref=slab_rows(me_r if j == 0 else chip(-j), h),
            send_sem=sib_send.at[h, j], recv_sem=sib_recv.at[h, j],
            device_id=(sibling, me_c), device_id_type=MESH,
        )

    for j in range(1, ncol):
        for i in range(units):
            send_ctx(j, i).start()
    for h in range(CHUNKS):
        for j in range(1, nz):
            send_doc(h, j).start()
        send_sibling(h, 0).start()

    def relay(h):
        for j in range(1, nz):
            send_doc(h, j).wait_recv()
            send_sibling(h, j).start()

    relay(0)
    for h in range(1, CHUNKS):
        for s in range(slots):
            load(h, s).start()
    own_coords.wait()
    own_counts.wait()
    for copy in own_docs + own_ctx:
        copy.wait()
    for j in range(1, ncol):
        for i in range(units):
            send_ctx(j, i).wait_recv()

    def multiply(h, s):
        load(h, s).wait()
        brows = slabs[h][coords[0, 1, 0, s]].astype(jnp.float32)
        first = coords[0, 2, 0, s] * per_block
        crows = jnp.concatenate([ctx_all[first + i] for i in range(per_block)], axis=0)
        crows = crows.reshape(BK // 16, 16, crows.shape[1])
        got = None
        for b in range(0, rows, PIECE):
            parts = []
            for i in range(b, b + PIECE):
                brow = jnp.broadcast_to(brows[i:i + 1, :], (16, brows.shape[1]))
                parts.append((crows * brow.astype(jnp.bfloat16)[None]).reshape(BK, brows.shape[1]))
            piece = jnp.dot(
                xbuf[s, :, h * depth + b * BK:h * depth + (b + PIECE) * BK],
                jnp.concatenate(parts, axis=0), preferred_element_type=jnp.float32,
            )
            got = piece if got is None else got + piece
        if h == 0:
            term[s] = got
        else:
            term[s] += got

    middle = (slots + 1) // 2
    for h in range(CHUNKS):
        for j in range(nz):
            send_sibling(h, j).wait_recv()

        def step(s, carry, h=h):
            multiply(h, s)
            return carry

        if h + 1 < CHUNKS:
            lax.fori_loop(0, middle, step, 0, unroll=True)
            relay(h + 1)
            lax.fori_loop(middle, slots, step, 0, unroll=True)
        else:
            lax.fori_loop(0, slots, step, 0, unroll=True)

    used = counts[0, 0]

    def partial_sum(q):
        total = jnp.zeros(own.shape, jnp.float32)
        for s in range(slots):
            wanted = jnp.logical_and(
                jnp.full(own.shape, coords[0, 0, 0, s]) == q, jnp.full(own.shape, used) > s
            )
            total += jnp.where(wanted, term[s], 0.0)
        return total

    def send_sum(j):
        return pltpu.make_async_remote_copy(
            src_ref=outbox.at[j], dst_ref=inbox.at[j - 1],
            send_sem=sum_send.at[j], recv_sem=sum_recv.at[j],
            device_id=(me_r, column(j)), device_id_type=MESH,
        )

    for j in range(1, ncol):
        outbox[j] = partial_sum(column(j)).astype(outbox.dtype)
        send_sum(j).start()
    own[...] = partial_sum(me_c)
    result = pltpu.make_async_copy(own, out, own_sem.at[0])
    result.start()
    for j in range(1, ncol):
        send_sum(j).wait_recv()
    result.wait()

    for j in range(1, ncol):
        for i in range(units):
            send_ctx(j, i).wait_send()
        send_sum(j).wait_send()
    for h in range(CHUNKS):
        for j in range(1, nz):
            send_doc(h, j).wait_send()
        for j in range(nz):
            send_sibling(h, j).wait_send()


def body(nrow, ncol, blocks, coords, counts, doc_factor, ctx_factor):
    slots, width = blocks.shape[2], blocks.shape[4]
    rank = doc_factor.shape[1]
    nz = nrow // 2
    unit = min(BK, ctx_factor.shape[0])
    units = ctx_factor.shape[0] // unit
    dma = pltpu.SemaphoreType.DMA
    own, inbox = pl.pallas_call(
        functools.partial(kernel, nrow, ncol),
        out_shape=(
            jax.ShapeDtypeStruct((BQ, rank), jnp.float32),
            jax.ShapeDtypeStruct((ncol - 1, BQ, rank), SEND),
        ),
        in_specs=[
            pl.BlockSpec(memory_space=pltpu.HBM),
            pl.BlockSpec(memory_space=pltpu.HBM),
            pl.BlockSpec(memory_space=pltpu.HBM),
            pl.BlockSpec(memory_space=pltpu.HBM),
            pl.BlockSpec(memory_space=pltpu.HBM),
        ],
        out_specs=(
            pl.BlockSpec(memory_space=pltpu.HBM),
            pl.BlockSpec(memory_space=pltpu.HBM),
        ),
        scratch_shapes=[
            pltpu.SMEM((1, 3, 1, slots), jnp.int32),
            pltpu.SMEM((1, 1), jnp.int32),
            pltpu.VMEM((slots, BQ, width), jnp.bfloat16),
            pltpu.VMEM((ctx_factor.shape[0] * ncol // unit, unit, rank), jnp.bfloat16),
            pltpu.VMEM((slots, BQ, rank), jnp.float32),
            pltpu.VMEM((ncol, BQ, rank), SEND),
            pltpu.VMEM((BQ, rank), jnp.float32),
            dma((CHUNKS, slots)),
            dma((2 + CHUNKS,)),
            dma((CHUNKS, nz)),
            dma((CHUNKS, nz)),
            dma((CHUNKS, nz)),
            dma((CHUNKS, nz)),
            dma((units,)),
            dma((ncol, units)),
            dma((ncol, units)),
            dma((ncol,)),
            dma((ncol,)),
        ] + [pltpu.VMEM((nrow, BD // CHUNKS, rank), jnp.bfloat16)] * CHUNKS,
        compiler_params=pltpu.CompilerParams(
            collective_id=0, has_side_effects=True, vmem_limit_bytes=60 * 1024 * 1024
        ),
        cost_estimate=pl.CostEstimate(
            flops=2 * slots * BQ * width * rank,
            bytes_accessed=slots * BQ * width * 2,
            transcendentals=0,
        ),
    )(blocks, coords.transpose(0, 3, 1, 2), counts, doc_factor, ctx_factor)
    for j in range(ncol - 1):
        own = own + inbox[j].astype(jnp.float32)
    return own


def solution(mesh):
    placed = (
        P("row", "col", None, None, None),
        P("row", "col", None, None),
        P("row", "col"),
        P(("col", "row"), None),
        P("col", None),
    )
    return jax.shard_map(
        functools.partial(body, mesh.shape["row"], mesh.shape["col"]),
        mesh=mesh, in_specs=placed, out_specs=P(("row", "col"), None), check_vma=False,
    )
```
